32 devices in a mesh: groups: 2 (over y), samp: 4 (over z), cent: 4 (over x, core).
Axes of the slice: x: 2, y: 2, z: 4, core: 2. Of those that a mesh axis runs over, the one named last changes fastest.
Arguments:
- samples: bfloat16 [8192, 1024], P(('groups', 'samp')), parts along dimension 0, may hold values from -16 to 16, as said below
- targets: float32 [8192], P(('groups', 'samp')), parts along dimension 0, may hold values from -2 to 4
- centres: bfloat16 [2048, 1024], P(('groups', 'cent')), parts along dimension 0, may hold values from -16 to 16, as said below
- tri_inv: float32 [2048, 1024], P(('groups', 'cent'), 'samp'), parts along dimension 0, as said below
- inner_inv: float32 [2048, 1024], P(('groups', 'cent'), 'samp'), parts along dimension 0, as said below
Outputs:
- fitted: float32 [8192], P(('groups', 'samp')), parts along dimension 0
The draws below stay inside these ranges and needn't reach their ends.
There are 2 independent parts, one for each index of `groups`. The reference program is written for one: setup_inputs(seed, part) draws one part's arguments, and reference() takes and returns one part's arrays. A program takes and returns all parts, laid end to end along the dimension named above; each array names one. Nothing has to cross between parts.
Inputs may be any that keep to these rules, and one draw needn't show every extreme that they name: `samples`: entries are rows of points with varying norms. `centres`: entries are rows of points with varying norms. `tri_inv`: upper triangular with a positive diagonal. `inner_inv`: upper triangular with a positive diagonal.
All inputs are finite; a program needn't handle non-finite values.
Results may differ from the reference program's by a relative error of at most 0.0003.
Values sent between devices are 32-bit elements; how exact they have to be, the bound alone decides.
A program may use at most 64 MiB of HBM per device.

```python
import math
import jax
import jax.numpy as jnp
from jax import lax

FEAT = 1024
ROWS_DEV = 1024
ITERS = 2
SAMPLES = 4096
CENTRES = 1024


noise_width = 2.0


def log_spread(key, count, lowest, highest):
    return jnp.exp(jax.random.uniform(key, (count, 1), jnp.float32, jnp.log(lowest), jnp.log(highest)))


def centre_points(key, bound, lowest, highest):
    key = jax.random.fold_in(key, 41)
    noise_key, scale_key = jax.random.split(key)
    noise = jnp.clip(jax.random.normal(noise_key, (CENTRES, FEAT), jnp.float32), -bound, bound)
    scales = log_spread(scale_key, CENTRES, lowest, highest)
    return noise * (noise_width * scales)


def triangle(key, diag_low, diag_high, off_scale):
    first_key, second_key = jax.random.split(key)
    row_ids = lax.broadcasted_iota(jnp.int32, (CENTRES, CENTRES), 0)
    col_ids = lax.broadcasted_iota(jnp.int32, (CENTRES, CENTRES), 1)
    upper = jnp.clip(jax.random.normal(first_key, (CENTRES, CENTRES), jnp.float32), -6.0, 6.0) * off_scale
    diagonal = jax.random.uniform(second_key, (CENTRES,), jnp.float32, diag_low, diag_high)
    return jnp.where(col_ids > row_ids, upper, 0.0) + jnp.diag(diagonal)


def draw_samples(key, part):
    centre_vals = centre_points(key, 4.0, 0.8, 1.25)
    key = jax.random.fold_in(key, 1)
    owner_key, fresh_key = jax.random.split(key)
    region_count = SAMPLES // ROWS_DEV
    region_size = CENTRES // region_count
    row_ids = lax.broadcasted_iota(jnp.int32, (SAMPLES,), 0)
    region = row_ids // ROWS_DEV
    owner = region * region_size + jax.random.randint(owner_key, (SAMPLES,), 0, region_size)
    position = region.astype(jnp.float32) / max(region_count - 1, 1)
    spread_sq = 0.1 + 0.55 * position
    fresh = jnp.clip(jax.random.normal(fresh_key, (SAMPLES, FEAT), jnp.float32), -4.0, 4.0)
    return (jnp.take(centre_vals, owner, axis=0) + jnp.sqrt(spread_sq)[:, None] * fresh).astype(jnp.bfloat16)


def draw_centres(key, part):
    return centre_points(key, 4.0, 0.8, 1.25).astype(jnp.bfloat16)


def draw_targets(key, part):
    key = jax.random.fold_in(key, 5)
    return 1.0 + 0.5 * jnp.clip(jax.random.normal(key, (SAMPLES,), jnp.float32), -6.0, 6.0)


def draw_tri_inv(key, part):
    key = jax.random.fold_in(key, 3)
    return triangle(key, 0.1 * CENTRES ** 0.5, 0.3 * CENTRES ** 0.5, 0.05)


def draw_inner_inv(key, part):
    key = jax.random.fold_in(key, 4)
    return triangle(key, 0.5, 2.0, 0.3 * CENTRES ** (-0.5))


def setup_inputs(seed: int = 0, part: int = 0) -> dict:
    splits = jax.random.split(jax.random.key(seed), 6)
    part_keys = jax.random.split(jax.random.fold_in(splits[5], part), 6)
    return {
        "samples": draw_samples(jax.random.fold_in(jax.random.fold_in(splits[5], part), 71), part),
        "targets": draw_targets(jax.random.fold_in(jax.random.fold_in(splits[5], part), 71), part),
        "centres": draw_centres(jax.random.fold_in(jax.random.fold_in(splits[5], part), 71), part),
        "tri_inv": draw_tri_inv(jax.random.fold_in(jax.random.fold_in(splits[5], part), 71), part),
        "inner_inv": draw_inner_inv(jax.random.fold_in(jax.random.fold_in(splits[5], part), 71), part),
    }


ridge_weight = 0.01
exact_mode = lax.Precision.HIGHEST


def reference(samples, targets, centres, tri_inv, inner_inv):
    centre_vals = centres.astype(jnp.float32)
    centre_norms = jnp.sum(centre_vals * centre_vals, axis=1)
    block_rows = math.gcd(SAMPLES, 4096)
    blocks = samples.reshape(SAMPLES // block_rows, block_rows, FEAT)

    def kernel_tile(sample_block):
        values = sample_block.astype(jnp.float32)
        crossed = jnp.dot(values, centre_vals.T, precision=exact_mode)
        row_norms = jnp.sum(values * values, axis=1)
        return jnp.exp((2.0 * crossed - row_norms[:, None] - centre_norms[None, :]) * (1.0 / FEAT))

    def kernel_rows(vector):
        outputs = lax.map(lambda sample_block: jnp.dot(kernel_tile(sample_block), vector, precision=exact_mode), blocks)
        return outputs.reshape(SAMPLES)

    def kernel_cols(vector):
        pieces = vector.reshape(SAMPLES // block_rows, block_rows)

        def advance(running, paired):
            sample_block, weight_block = paired
            return running + jnp.dot(weight_block, kernel_tile(sample_block), precision=exact_mode), None

        return lax.scan(advance, jnp.zeros((CENTRES,), jnp.float32), (blocks, pieces))[0]

    def forward(matrix, vector):
        return jnp.dot(matrix, vector, precision=exact_mode)

    def backward(matrix, vector):
        return jnp.dot(vector, matrix, precision=exact_mode)

    def operator(vector):
        lifted = forward(inner_inv, vector)
        expanded = forward(tri_inv, lifted)
        row_values = kernel_rows(expanded)
        column_values = kernel_cols(row_values)
        combined = backward(tri_inv, column_values) / SAMPLES + ridge_weight * lifted
        return backward(inner_inv, combined)

    rhs = backward(inner_inv, backward(tri_inv, kernel_cols(targets)) / SAMPLES)
    solution = jnp.zeros((CENTRES,), jnp.float32)
    residual = rhs
    direction = rhs
    norm_now = jnp.sum(residual * residual)
    for advance_index in range(ITERS):
        mapped = operator(direction)
        step_size = norm_now / jnp.sum(direction * mapped)
        solution = solution + step_size * direction
        residual = residual - step_size * mapped
        norm_next = jnp.sum(residual * residual)
        direction = residual + (norm_next / norm_now) * direction
        norm_now = norm_next
    coefficients = forward(tri_inv, forward(inner_inv, solution))
    return kernel_rows(coefficients)
```

```python
import functools
import jax
import jax.numpy as jnp
from jax import lax
from jax.experimental import pallas as pl
from jax.experimental.pallas import tpu as pltpu
from jax.sharding import PartitionSpec as P

ITERS = 2
ridge_weight = 0.01
MESH = pl.DeviceIdType.MESH
LANES = 128


def row_to_col(row):
    width = row.shape[1]
    r = lax.broadcasted_iota(jnp.int32, (width, width), 0)
    c = lax.broadcasted_iota(jnp.int32, (width, width), 1)
    return jnp.sum(jnp.where(r == c, row, 0.0), axis=1, keepdims=True)


def col_to_row(col):
    width = col.shape[0]
    r = lax.broadcasted_iota(jnp.int32, (width, width), 0)
    c = lax.broadcasted_iota(jnp.int32, (width, width), 1)
    return jnp.sum(jnp.where(r == c, col, 0.0), axis=0, keepdims=True)


def kernel(n_s, n_c, split, samples_hbm, targets, centres, tri, inner, fitted,
           samples, ktile, tri_row, inner_t, joined,
           col_buf, rhs_buf, vec_buf, row_buf, all_buf,
           load_sem, tri_sem, chain_send, chain_recv, send_sem, recv_sem):
    g = lax.axis_index("groups")
    s = lax.axis_index("samp")
    c = lax.axis_index("cent")
    n = n_s * n_c
    me = s * n_c + c
    cb, feat = centres.shape
    rb = samples_hbm.shape[0]
    sb = inner_t.shape[0]
    total = tri_row.shape[1]
    part = sb // n_c
    total_rows = float(rb * n_s)
    chunk = min(256, rb)
    chunks = rb // chunk

    def at(ss, cc):
        return {"groups": g, "samp": ss, "cent": cc}

    def each(count, act):
        if count <= 16:
            for i in range(1, count):
                act(i)
        else:
            lax.fori_loop(1, count, lambda i, z: (act(i), z)[1], 0)

    def peers(kind, act):
        if kind == "samp":
            each(n_s, lambda i: act(lax.rem(s + i, n_s), c))
        elif kind == "cent":
            each(n_c, lambda i: act(s, lax.rem(c + i, n_c)))
        else:
            each(n, lambda i: act(lax.rem(s + i // n_c, n_s), lax.rem(c + i % n_c, n_c)))

    def loads(j):
        rows = pl.ds(j * chunk, chunk)
        return pltpu.make_async_copy(samples_hbm.at[rows], samples.at[rows], load_sem.at[j])

    barrier = pltpu.get_barrier_semaphore()
    peers("all", lambda a, b: pl.semaphore_signal(barrier, inc=1, device_id=at(a, b), device_id_type=MESH))
    for j in range(chunks):
        loads(j).start()

    def live(k):
        return (k + 1) * sb > c * cb

    def tri_block(k):
        return tri_row.at[:, pl.ds(pl.multiple_of(k * sb, LANES), sb)]

    def inner_slot(k):
        return joined.at[:, pl.ds(pl.multiple_of(k * cb, LANES), cb)]

    if split:
        own_tri = pltpu.make_async_copy(tri, tri_block(s), tri_sem.at[0])
        own_tri.start()
        inner_t[...] = inner[...].T
        for k in range(n_s):
            @pl.when(jnp.logical_not(live(k)) & (k != s))
            def _():
                tri_row[:, k * sb:(k + 1) * sb] = jnp.zeros((cb, sb), jnp.float32)
    else:
        own_tri = pltpu.make_async_copy(tri, tri_row, tri_sem.at[0])
        own_tri.start()
        inner_t[...] = inner[...]

    centre_vals = centres[...]
    wide = centre_vals.astype(jnp.float32)
    centre_norms = jnp.sum(wide * wide, axis=1, keepdims=True)

    def tile(j):
        loads(j).wait()
        block = samples[j * chunk:(j + 1) * chunk, :]
        wide_block = block.astype(jnp.float32)
        norms = col_to_row(jnp.sum(wide_block * wide_block, axis=1, keepdims=True))
        crossed = lax.dot_general(centre_vals, block, (((1,), (1,)), ((), ())),
                                  preferred_element_type=jnp.float32)
        ktile[:, j * chunk:(j + 1) * chunk] = jnp.exp((2.0 * crossed - norms - centre_norms) * (1.0 / feat))

    def hop(way, j):
        k = s - way * j
        lane = (1 - way) // 2
        return pltpu.make_async_remote_copy(
            src_ref=tri_block(k), dst_ref=tri_block(k),
            send_sem=chain_send.at[lane, j], recv_sem=chain_recv.at[lane, j],
            device_id=at(s + way, c), device_id_type=MESH)

    def inside(k):
        return (k >= 0) & (k < n_s)

    def chain_start(j):
        for way in (1, -1):
            k = s - way * j

            @pl.when(inside(k) & inside(s + way) & live(k))
            def _():
                hop(way, j).start()

    def chain_wait(j):
        for way in (1, -1):
            k = s - way * j
            lane = (1 - way) // 2

            @pl.when(inside(k) & live(k))
            def _():
                pltpu.make_async_copy(tri_block(k), tri_block(k), chain_recv.at[lane, j - 1]).wait()

    def chain_finish():
        for j in range(n_s - 1):
            for way in (1, -1):
                k = s - way * j

                @pl.when(inside(k) & inside(s + way) & live(k))
                def _():
                    hop(way, j).wait_send()

    def publish(buf, slot, index, kind):
        peers(kind, lambda a, b: pltpu.make_async_remote_copy(
            src_ref=buf.at[slot], dst_ref=buf.at[slot],
            send_sem=send_sem.at[index], recv_sem=recv_sem.at[index],
            device_id=at(a, b), device_id_type=MESH).start())

    def arrive(buf, index):
        rest = buf.at[pl.ds(0, buf.shape[0] - 1)]
        pltpu.make_async_copy(rest, rest, recv_sem.at[index]).wait()

    def settle(buf, index):
        rest = buf.at[pl.ds(0, buf.shape[0] - 1)]
        pltpu.make_async_copy(rest, rest, send_sem.at[index]).wait()

    def summed(buf, first=0, count=None):
        count = buf.shape[0] if count is None else count
        if count <= 32:
            acc = buf[first]
            for i in range(1, count):
                acc = acc + buf[first + i]
            return acc
        return lax.fori_loop(1, count, lambda i, acc: acc + buf[first + i], buf[first])

    def tail(value):
        return jnp.broadcast_to(value, (1, LANES))

    def square(vector):
        return jnp.sum(vector * vector, axis=1, keepdims=True)

    half = chunks // 2
    for j in range(half):
        tile(j)
    pl.semaphore_wait(barrier, n - 1)
    own_tri.wait()
    if split:
        chain_start(0)

    def inner_copy(i):
        other = lax.rem(c + i, n_c)
        return pltpu.make_async_remote_copy(
            src_ref=inner_t.at[pl.ds(pl.multiple_of(other * part, 8), part)], dst_ref=inner_slot(c),
            send_sem=tri_sem.at[1], recv_sem=tri_sem.at[2],
            device_id=at(s, other), device_id_type=MESH)

    for i in range(1, n_c):
        inner_copy(i).start()
    own_inner = pltpu.make_async_copy(
        inner_t.at[pl.ds(pl.multiple_of(c * part, 8), part)], inner_slot(c), tri_sem.at[3])
    own_inner.start()
    for j in range(half, chunks):
        tile(j)

    aimed = jnp.sum(ktile[...] * targets[...], axis=1, keepdims=True)
    if split:
        col_buf[s] = col_to_row(aimed)
        publish(col_buf, s, 0, "samp")
        if n_s > 1:
            chain_wait(1)
            if n_s > 2:
                chain_start(1)
        arrive(col_buf, 0)
        pulled = row_to_col(summed(col_buf))
        own_block = tri_row[:, pl.ds(pl.multiple_of(s * sb, LANES), sb)]
        rhs_buf[me] = jnp.sum(own_block * pulled, axis=0, keepdims=True)
        publish(rhs_buf, me, 1, "all")
        for j in range(2, n_s):
            chain_wait(j)
            if j < n_s - 1:
                chain_start(j)
        arrive(rhs_buf, 1)
        rh = jnp.concatenate([summed(rhs_buf, k * n_c, n_c) for k in range(n_s)], axis=1)
    else:
        rhs_buf[me] = jnp.sum(tri_row[...] * aimed, axis=0, keepdims=True)
        publish(rhs_buf, me, 1, "all")
        arrive(rhs_buf, 1)
        rh = summed(rhs_buf)
    rh = rh / total_rows

    moved = inner_t.at[pl.ds(0, (n_c - 1) * part)]
    pltpu.make_async_copy(moved, moved, tri_sem.at[2]).wait()
    own_inner.wait()

    def condition(vector, buf, index):
        picked = jnp.sum(joined[...] * vector, axis=1, keepdims=True)
        buf[me, :, :total] = jnp.sum(joined[...] * picked, axis=0, keepdims=True)
        buf[me, :, total:] = tail(jnp.sum(picked * picked, axis=0, keepdims=True))
        publish(buf, me, index, "all")
        arrive(buf, index)
        got = summed(buf)
        return got[:, :total], got[:, total:total + 1]

    def rows_part(lifted):
        expanded = jnp.sum(tri_row[...] * lifted, axis=1, keepdims=True)
        return jnp.sum(ktile[...] * expanded, axis=0, keepdims=True)

    lifted, norm_now = condition(rh, vec_buf.at[0], 2)
    kept = jnp.zeros((1, rb), jnp.float32)
    for turn in range(ITERS - 1):
        base = 3 + 3 * turn
        rows_buf = row_buf.at[turn]
        rows_buf[c] = rows_part(lifted)
        publish(rows_buf, c, base, "cent")
        arrive(rows_buf, base)
        rows = summed(rows_buf)
        columns = jnp.sum(ktile[...] * rows, axis=1, keepdims=True)
        buf = vec_buf.at[1 + 2 * turn]
        buf[me, :, :total] = jnp.sum(tri_row[...] * columns, axis=0, keepdims=True)
        buf[me, :, total:] = tail(square(rows) / n_c)
        publish(buf, me, base + 1, "all")
        arrive(buf, base + 1)
        got = summed(buf)
        mapped = got[:, :total] / total_rows + ridge_weight * lifted
        energy = got[:, total:total + 1] / total_rows + ridge_weight * square(lifted)
        step_size = norm_now / energy
        kept = kept + step_size * rows
        rh = rh - step_size * mapped
        fresh, norm_next = condition(rh, vec_buf.at[2 + 2 * turn], base + 2)
        lifted = fresh + (norm_next / norm_now) * lifted
        norm_now = norm_next

    last = 3 * ITERS
    all_buf[me] = rows_part(lifted)
    publish(all_buf, me, last, "all")
    arrive(all_buf, last)
    if n_s <= 8:
        energy = jnp.zeros((1, 1), jnp.float32)
        for k in range(n_s):
            energy = energy + square(summed(all_buf, k * n_c, n_c))
    else:
        energy = lax.fori_loop(
            0, n_s, lambda k, acc: acc + square(summed(all_buf, k * n_c, n_c)), jnp.zeros((1, 1), jnp.float32))
    rows = summed(all_buf, s * n_c, n_c)
    step_size = norm_now / (energy / total_rows + ridge_weight * square(lifted))
    fitted[...] = kept + step_size * rows

    pltpu.make_async_copy(moved, moved, tri_sem.at[1]).wait()
    if split:
        chain_finish()
        settle(col_buf, 0)
    settle(rhs_buf, 1)
    settle(vec_buf.at[0], 2)
    for turn in range(ITERS - 1):
        base = 3 + 3 * turn
        settle(row_buf.at[turn], base)
        settle(vec_buf.at[1 + 2 * turn], base + 1)
        settle(vec_buf.at[2 + 2 * turn], base + 2)
    settle(all_buf, last)


def body(samples, targets, centres, tri_inv, inner_inv):
    n_s, n_c = lax.axis_size("samp"), lax.axis_size("cent")
    n = n_s * n_c
    rb, feat = samples.shape
    cb = centres.shape[0]
    sb = tri_inv.shape[1]
    total = sb * n_s
    split = sb % LANES == 0
    if split:
        tri, inner = tri_inv, inner_inv
    else:
        tri, inner = lax.all_gather(tri_inv, "samp", axis=1, tiled=True), inner_inv.T
    chunks = rb // min(256, rb)
    wide = total + LANES
    f32 = jnp.float32
    vmem = pl.BlockSpec(memory_space=pltpu.VMEM)
    hbm = pl.BlockSpec(memory_space=pl.ANY)
    out = pl.pallas_call(
        functools.partial(kernel, n_s, n_c, split),
        out_shape=jax.ShapeDtypeStruct((1, rb), f32),
        in_specs=[hbm, vmem, vmem, hbm, vmem],
        out_specs=vmem,
        scratch_shapes=[
            pltpu.VMEM((rb, feat), samples.dtype),
            pltpu.VMEM((cb, rb), f32),
            pltpu.VMEM((cb, total), f32),
            pltpu.VMEM((sb, cb), f32),
            pltpu.VMEM((sb // n_c, total), f32),
            pltpu.VMEM((n_s, 1, cb), f32),
            pltpu.VMEM((n, 1, sb if split else total), f32),
            pltpu.VMEM((2 * ITERS - 1, n, 1, wide), f32),
            pltpu.VMEM((ITERS - 1, n_c, 1, rb), f32),
            pltpu.VMEM((n, 1, rb), f32),
            pltpu.SemaphoreType.DMA((chunks,)),
            pltpu.SemaphoreType.DMA((4,)),
            pltpu.SemaphoreType.DMA((2, n_s)),
            pltpu.SemaphoreType.DMA((2, n_s)),
            pltpu.SemaphoreType.DMA((3 * ITERS + 1,)),
            pltpu.SemaphoreType.DMA((3 * ITERS + 1,)),
        ],
        compiler_params=pltpu.CompilerParams(
            collective_id=0, has_side_effects=True, vmem_limit_bytes=48 * 2 ** 20),
    )(samples, targets.reshape(1, rb), centres, tri, inner)
    return out.reshape(rb)


def solution(mesh):
    in_specs = (
        P(("groups", "samp"), None),
        P(("groups", "samp")),
        P(("groups", "cent"), None),
        P(("groups", "cent"), "samp"),
        P(("groups", "cent"), "samp"),
    )
    out_specs = P(("groups", "samp"))
    return jax.shard_map(body, mesh=mesh, in_specs=in_specs, out_specs=out_specs, check_vma=False)
```

```python
import functools
import jax
import jax.numpy as jnp
from jax import lax
from jax.experimental import pallas as pl
from jax.experimental.pallas import tpu as pltpu
from jax.sharding import PartitionSpec as P

ITERS = 2
ridge_weight = 0.01
FIRST_BACK_JOINED = True
LAST_JOINED = True
JOINED = FIRST_BACK_JOINED or LAST_JOINED
MESH = pl.DeviceIdType.MESH
LANES = 128


def row_to_col(row):
    width = row.shape[1]
    r = lax.broadcasted_iota(jnp.int32, (width, width), 0)
    c = lax.broadcasted_iota(jnp.int32, (width, width), 1)
    return jnp.sum(jnp.where(r == c, row, 0.0), axis=1, keepdims=True)


def col_to_row(col):
    width = col.shape[0]
    r = lax.broadcasted_iota(jnp.int32, (width, width), 0)
    c = lax.broadcasted_iota(jnp.int32, (width, width), 1)
    return jnp.sum(jnp.where(r == c, col, 0.0), axis=0, keepdims=True)


def kernel(n_s, n_c, split, samples_hbm, targets_hbm, centres_hbm, tri, inner_hbm, fitted,
           samples, targets, centres, inner, ktile, tri_row, inner_t, joined,
           lifted_ref, col_buf, rhs_buf, vec_buf, row_buf, all_buf,
           load_sem, tri_sem, chain_send, chain_recv, send_sem, recv_sem):
    g = lax.axis_index("groups")
    s = lax.axis_index("samp")
    c = lax.axis_index("cent")
    n = n_s * n_c
    me = s * n_c + c
    cb, feat = centres.shape
    rb = samples_hbm.shape[0]
    sb = inner_t.shape[0]
    total = tri_row.shape[1]
    part = sb // n_c
    total_rows = float(rb * n_s)
    chunk = min(256, rb)
    chunks = rb // chunk

    def at(ss, cc):
        return {"groups": g, "samp": ss, "cent": cc}

    def each(count, act):
        if count <= 16:
            for i in range(1, count):
                act(i)
        else:
            lax.fori_loop(1, count, lambda i, z: (act(i), z)[1], 0)

    def peers(kind, act):
        if kind == "samp":
            each(n_s, lambda i: act(lax.rem(s + i, n_s), c))
        elif kind == "cent":
            each(n_c, lambda i: act(s, lax.rem(c + i, n_c)))
        else:
            each(n, lambda i: act(lax.rem(s + i // n_c, n_s), lax.rem(c + i % n_c, n_c)))

    def loads(j):
        rows = pl.ds(j * chunk, chunk)
        return pltpu.make_async_copy(samples_hbm.at[rows], samples.at[rows], load_sem.at[j])

    barrier = pltpu.get_barrier_semaphore()
    peers("all", lambda a, b: pl.semaphore_signal(barrier, inc=1, device_id=at(a, b), device_id_type=MESH))
    load_inner = pltpu.make_async_copy(inner_hbm, inner, load_sem.at[chunks])
    load_centres = pltpu.make_async_copy(centres_hbm, centres, load_sem.at[chunks + 1])
    load_targets = pltpu.make_async_copy(targets_hbm, targets, load_sem.at[chunks + 2])
    load_centres.start()
    for j in range(chunks):
        loads(j).start()
        if j == 0:
            load_inner.start()
    load_targets.start()

    def live(k):
        return (k + 1) * sb > c * cb

    def tri_block(k):
        return tri_row.at[:, pl.ds(pl.multiple_of(k * sb, LANES), sb)]

    def inner_slot(k):
        return joined.at[:, pl.ds(pl.multiple_of(k * cb, LANES), cb)]

    if split:
        own_tri = pltpu.make_async_copy(tri, tri_block(s), tri_sem.at[0])
        own_tri.start()
        load_inner.wait()
        inner_t[...] = inner[...].T
        for k in range(n_s):
            @pl.when(jnp.logical_not(live(k)) & (k != s))
            def _():
                tri_row[:, k * sb:(k + 1) * sb] = jnp.zeros((cb, sb), jnp.float32)
    else:
        own_tri = pltpu.make_async_copy(tri, tri_row, tri_sem.at[0])
        own_tri.start()
        load_inner.wait()
        inner_t[...] = inner[...]

    load_centres.wait()
    centre_vals = centres[...]
    wide = centre_vals.astype(jnp.float32)
    centre_norms = jnp.sum(wide * wide, axis=1, keepdims=True)

    def tile(j):
        loads(j).wait()
        block = samples[j * chunk:(j + 1) * chunk, :]
        wide_block = block.astype(jnp.float32)
        norms = col_to_row(jnp.sum(wide_block * wide_block, axis=1, keepdims=True))
        crossed = lax.dot_general(centre_vals, block, (((1,), (1,)), ((), ())),
                                  preferred_element_type=jnp.float32)
        ktile[:, j * chunk:(j + 1) * chunk] = jnp.exp((2.0 * crossed - norms - centre_norms) * (1.0 / feat))

    def hop(way, j):
        k = s - way * j
        lane = (1 - way) // 2
        return pltpu.make_async_remote_copy(
            src_ref=tri_block(k), dst_ref=tri_block(k),
            send_sem=chain_send.at[lane, j], recv_sem=chain_recv.at[lane, j],
            device_id=at(s + way, c), device_id_type=MESH)

    def inside(k):
        return (k >= 0) & (k < n_s)

    def chain_start(j):
        for way in (1, -1):
            k = s - way * j

            @pl.when(inside(k) & inside(s + way) & live(k))
            def _():
                hop(way, j).start()

    def chain_wait(j):
        for way in (1, -1):
            k = s - way * j
            lane = (1 - way) // 2

            @pl.when(inside(k) & live(k))
            def _():
                pltpu.make_async_copy(tri_block(k), tri_block(k), chain_recv.at[lane, j - 1]).wait()

    def chain_finish():
        for j in range(n_s - 1):
            for way in (1, -1):
                k = s - way * j

                @pl.when(inside(k) & inside(s + way) & live(k))
                def _():
                    hop(way, j).wait_send()

    def publish(buf, slot, index, kind):
        peers(kind, lambda a, b: pltpu.make_async_remote_copy(
            src_ref=buf.at[slot], dst_ref=buf.at[slot],
            send_sem=send_sem.at[index], recv_sem=recv_sem.at[index],
            device_id=at(a, b), device_id_type=MESH).start())

    def arrive(buf, index):
        rest = buf.at[pl.ds(0, buf.shape[0] - 1)]
        pltpu.make_async_copy(rest, rest, recv_sem.at[index]).wait()

    def settle(buf, index):
        rest = buf.at[pl.ds(0, buf.shape[0] - 1)]
        pltpu.make_async_copy(rest, rest, send_sem.at[index]).wait()

    def summed(buf, first=0, count=None):
        count = buf.shape[0] if count is None else count
        if count <= 32:
            acc = buf[first]
            for i in range(1, count):
                acc = acc + buf[first + i]
            return acc
        return lax.fori_loop(1, count, lambda i, acc: acc + buf[first + i], buf[first])

    def tail(value):
        return jnp.broadcast_to(value, (1, LANES))

    def square(vector):
        return jnp.sum(vector * vector, axis=1, keepdims=True)

    half = chunks // 2
    for j in range(half):
        tile(j)
    pl.semaphore_wait(barrier, n - 1)
    own_tri.wait()
    if split and JOINED:
        chain_start(0)

    def inner_copy(i):
        other = lax.rem(c + i, n_c)
        return pltpu.make_async_remote_copy(
            src_ref=inner_t.at[pl.ds(pl.multiple_of(other * part, 8), part)], dst_ref=inner_slot(c),
            send_sem=tri_sem.at[1], recv_sem=tri_sem.at[2],
            device_id=at(s, other), device_id_type=MESH)

    for i in range(1, n_c):
        inner_copy(i).start()
    own_inner = pltpu.make_async_copy(
        inner_t.at[pl.ds(pl.multiple_of(c * part, 8), part)], inner_slot(c), tri_sem.at[3])
    own_inner.start()
    for j in range(half, chunks):
        tile(j)

    load_targets.wait()
    aimed = jnp.sum(ktile[...] * targets[...], axis=1, keepdims=True)

    def over_samp(col, slot, index, between=None):
        buf = col_buf.at[slot]
        buf[s] = col_to_row(col)
        publish(buf, s, index, "samp")
        if between is not None:
            between()
        arrive(buf, index)
        return row_to_col(summed(buf))

    def own_block():
        return tri_row[:, pl.ds(pl.multiple_of(s * sb, LANES), sb)]

    def pull_blocks(col, scalar, slot, index, between=None):
        buf = rhs_buf.at[slot]
        buf[me, :, :sb] = jnp.sum(own_block() * col, axis=0, keepdims=True)
        buf[me, :, sb:] = tail(scalar)
        publish(buf, me, index, "all")
        if between is not None:
            between()
        arrive(buf, index)
        blocks = [summed(buf, k * n_c, n_c) for k in range(n_s)]
        scalar = blocks[0][:, sb:sb + 1]
        for k in range(1, n_s):
            scalar = scalar + blocks[k][:, sb:sb + 1]
        return jnp.concatenate([block[:, :sb] for block in blocks], axis=1), scalar

    def chain_step(j):
        if split and JOINED and 0 < j < n_s:
            chain_wait(j)
            if j < n_s - 1:
                chain_start(j)

    extra = 3 * ITERS + 1
    zero = jnp.zeros((1, 1), jnp.float32)
    if split:
        pulled = over_samp(aimed, 0, 0)
        rh, _ = pull_blocks(pulled, zero, 0, 1, lambda: chain_step(1))
    else:
        buf = rhs_buf.at[0]
        buf[me] = jnp.sum(tri_row[...] * aimed, axis=0, keepdims=True)
        publish(buf, me, 1, "all")
        arrive(buf, 1)
        rh = summed(buf)
    rh = rh / total_rows

    moved = inner_t.at[pl.ds(0, (n_c - 1) * part)]
    pltpu.make_async_copy(moved, moved, tri_sem.at[2]).wait()
    own_inner.wait()

    def condition(vector, buf, index, between=None):
        picked = jnp.sum(joined[...] * vector, axis=1, keepdims=True)
        buf[me, :, :total] = jnp.sum(joined[...] * picked, axis=0, keepdims=True)
        buf[me, :, total:] = tail(jnp.sum(picked * picked, axis=0, keepdims=True))
        publish(buf, me, index, "all")
        if between is not None:
            between()
        arrive(buf, index)
        got = summed(buf)
        return got[:, :total], got[:, total:total + 1]

    def rows_part(lifted, joined_rows, slot, index, between=None):
        if joined_rows:
            expanded = jnp.sum(tri_row[...] * lifted, axis=1, keepdims=True)
        else:
            lifted_ref[...] = lifted
            mine = lifted_ref[:, pl.ds(pl.multiple_of(s * sb, LANES), sb)]
            expanded = over_samp(jnp.sum(own_block() * mine, axis=1, keepdims=True), slot, index, between)
        return jnp.sum(ktile[...] * expanded, axis=0, keepdims=True)

    lifted, norm_now = condition(rh, vec_buf.at[0], 2, lambda: chain_step(2))
    kept = jnp.zeros((1, rb), jnp.float32)
    for turn in range(ITERS - 1):
        base = 3 + 3 * turn
        rows_buf = row_buf.at[turn]
        first = split and turn == 0
        rows_buf[c] = rows_part(lifted, not first, 1, extra)
        publish(rows_buf, c, base, "cent")
        arrive(rows_buf, base)
        rows = summed(rows_buf)
        columns = jnp.sum(ktile[...] * rows, axis=1, keepdims=True)
        if first:
            for j in range(3, n_s):
                chain_step(j)
        if first and not FIRST_BACK_JOINED:
            columns = over_samp(columns, 2, extra + 1)
            back, scalar = pull_blocks(columns, square(rows) / n_c, 1, base + 1)
        else:
            buf = vec_buf.at[1 + 2 * turn]
            buf[me, :, :total] = jnp.sum(tri_row[...] * columns, axis=0, keepdims=True)
            buf[me, :, total:] = tail(square(rows) / n_c)
            publish(buf, me, base + 1, "all")
            arrive(buf, base + 1)
            got = summed(buf)
            back, scalar = got[:, :total], got[:, total:total + 1]
        mapped = back / total_rows + ridge_weight * lifted
        energy = scalar / total_rows + ridge_weight * square(lifted)
        step_size = norm_now / energy
        kept = kept + step_size * rows
        rh = rh - step_size * mapped
        fresh, norm_next = condition(rh, vec_buf.at[2 + 2 * turn], base + 2)
        lifted = fresh + (norm_next / norm_now) * lifted
        norm_now = norm_next

    last = 3 * ITERS
    all_buf[me] = rows_part(lifted, not split or LAST_JOINED, 3, extra + 2)
    publish(all_buf, me, last, "all")
    arrive(all_buf, last)
    if n_s <= 8:
        energy = jnp.zeros((1, 1), jnp.float32)
        for k in range(n_s):
            energy = energy + square(summed(all_buf, k * n_c, n_c))
    else:
        energy = lax.fori_loop(
            0, n_s, lambda k, acc: acc + square(summed(all_buf, k * n_c, n_c)), jnp.zeros((1, 1), jnp.float32))
    rows = summed(all_buf, s * n_c, n_c)
    step_size = norm_now / (energy / total_rows + ridge_weight * square(lifted))
    fitted[...] = kept + step_size * rows

    pltpu.make_async_copy(moved, moved, tri_sem.at[1]).wait()
    if split:
        if JOINED:
            chain_finish()
        settle(col_buf.at[0], 0)
        settle(col_buf.at[1], extra)
        if not FIRST_BACK_JOINED:
            settle(col_buf.at[2], extra + 1)
        if not LAST_JOINED:
            settle(col_buf.at[3], extra + 2)
    settle(rhs_buf.at[0], 1)
    settle(vec_buf.at[0], 2)
    for turn in range(ITERS - 1):
        base = 3 + 3 * turn
        settle(row_buf.at[turn], base)
        if split and turn == 0 and not FIRST_BACK_JOINED:
            settle(rhs_buf.at[1], base + 1)
        else:
            settle(vec_buf.at[1 + 2 * turn], base + 1)
        settle(vec_buf.at[2 + 2 * turn], base + 2)
    settle(all_buf, last)


def body(samples, targets, centres, tri_inv, inner_inv):
    n_s, n_c = lax.axis_size("samp"), lax.axis_size("cent")
    n = n_s * n_c
    rb, feat = samples.shape
    cb = centres.shape[0]
    sb = tri_inv.shape[1]
    total = sb * n_s
    split = sb % LANES == 0
    if split:
        tri, inner = tri_inv, inner_inv
    else:
        tri, inner = lax.all_gather(tri_inv, "samp", axis=1, tiled=True), inner_inv.T
    chunks = rb // min(256, rb)
    wide = total + LANES
    f32 = jnp.float32
    vmem = pl.BlockSpec(memory_space=pltpu.VMEM)
    hbm = pl.BlockSpec(memory_space=pltpu.HBM)
    out = pl.pallas_call(
        functools.partial(kernel, n_s, n_c, split),
        out_shape=jax.ShapeDtypeStruct((1, rb), f32),
        in_specs=[hbm] * 5,
        out_specs=vmem,
        scratch_shapes=[
            pltpu.VMEM((rb, feat), samples.dtype),
            pltpu.VMEM((1, rb), f32),
            pltpu.VMEM((cb, feat), centres.dtype),
            pltpu.VMEM(inner.shape, f32),
            pltpu.VMEM((cb, rb), f32),
            pltpu.VMEM((cb, total), f32),
            pltpu.VMEM((sb, cb), f32),
            pltpu.VMEM((sb // n_c, total), f32),
            pltpu.VMEM((1, total), f32),
            pltpu.VMEM((4, n_s, 1, cb), f32),
            pltpu.VMEM((2, n, 1, sb + LANES if split else total), f32),
            pltpu.VMEM((2 * ITERS - 1, n, 1, wide), f32),
            pltpu.VMEM((ITERS - 1, n_c, 1, rb), f32),
            pltpu.VMEM((n, 1, rb), f32),
            pltpu.SemaphoreType.DMA((chunks + 3,)),
            pltpu.SemaphoreType.DMA((4,)),
            pltpu.SemaphoreType.DMA((2, n_s)),
            pltpu.SemaphoreType.DMA((2, n_s)),
            pltpu.SemaphoreType.DMA((3 * ITERS + 4,)),
            pltpu.SemaphoreType.DMA((3 * ITERS + 4,)),
        ],
        compiler_params=pltpu.CompilerParams(
            collective_id=0, has_side_effects=True, vmem_limit_bytes=60 * 2 ** 20),
    )(samples, targets.reshape(1, rb), centres, tri, inner)
    return out.reshape(rb)


def solution(mesh):
    in_specs = (
        P(("groups", "samp"), None),
        P(("groups", "samp")),
        P(("groups", "cent"), None),
        P(("groups", "cent"), "samp"),
        P(("groups", "cent"), "samp"),
    )
    out_specs = P(("groups", "samp"))
    return jax.shard_map(body, mesh=mesh, in_specs=in_specs, out_specs=out_specs, check_vma=False)
```

```python
import functools
import jax
import jax.numpy as jnp
from jax import lax
from jax.experimental import pallas as pl
from jax.experimental.pallas import tpu as pltpu
from jax.sharding import PartitionSpec as P

ITERS = 2
ridge_weight = 0.01
FIRST_BACK_JOINED = True
LAST_JOINED = True
PIECES = 1
JOINED = FIRST_BACK_JOINED or LAST_JOINED
MESH = pl.DeviceIdType.MESH
LANES = 128


def row_to_col(row):
    width = row.shape[1]
    r = lax.broadcasted_iota(jnp.int32, (width, width), 0)
    c = lax.broadcasted_iota(jnp.int32, (width, width), 1)
    return jnp.sum(jnp.where(r == c, row, 0.0), axis=1, keepdims=True)


def col_to_row(col):
    width = col.shape[0]
    r = lax.broadcasted_iota(jnp.int32, (width, width), 0)
    c = lax.broadcasted_iota(jnp.int32, (width, width), 1)
    return jnp.sum(jnp.where(r == c, col, 0.0), axis=0, keepdims=True)


def kernel(n_s, n_c, split, samples_hbm, targets_hbm, centres_hbm, tri, inner_hbm, fitted,
           samples, targets, centres, inner, ktile, tri_row, inner_t, joined,
           lifted_ref, col_buf, rhs_buf, vec_buf, row_buf, all_buf,
           load_sem, tri_sem, chain_send, chain_recv, send_sem, recv_sem):
    g = lax.axis_index("groups")
    s = lax.axis_index("samp")
    c = lax.axis_index("cent")
    n = n_s * n_c
    me = s * n_c + c
    cb, feat = centres.shape
    rb = samples_hbm.shape[0]
    sb = inner_t.shape[0]
    total = tri_row.shape[1]
    part = sb // n_c
    total_rows = float(rb * n_s)
    chunk = min(256, rb)
    chunks = rb // chunk

    def at(ss, cc):
        return {"groups": g, "samp": ss, "cent": cc}

    def each(count, order, act):
        if count <= 16:
            for i in order:
                act(i)
        else:
            lax.fori_loop(1, count, lambda i, z: (act(i), z)[1], 0)

    def reach(i):
        a, b = i // n_c, i % n_c
        return (max(a, n_s - a) if a else 0) + (1 if b > 1 else 0)

    far_first = sorted(range(1, n), key=lambda i: -reach(i))

    def peers(kind, act):
        if kind == "samp":
            each(n_s, sorted(range(1, n_s), key=lambda i: -max(i, n_s - i)), lambda i: act(lax.rem(s + i, n_s), c))
        elif kind == "cent":
            each(n_c, range(1, n_c), lambda i: act(s, lax.rem(c + i, n_c)))
        else:
            each(n, far_first, lambda i: act(lax.rem(s + i // n_c, n_s), lax.rem(c + i % n_c, n_c)))

    def loads(j):
        rows = pl.ds(j * chunk, chunk)
        return pltpu.make_async_copy(samples_hbm.at[rows], samples.at[rows], load_sem.at[j])

    barrier = pltpu.get_barrier_semaphore()
    peers("all", lambda a, b: pl.semaphore_signal(barrier, inc=1, device_id=at(a, b), device_id_type=MESH))
    load_inner = pltpu.make_async_copy(inner_hbm, inner, load_sem.at[chunks])
    load_centres = pltpu.make_async_copy(centres_hbm, centres, load_sem.at[chunks + 1])
    load_targets = pltpu.make_async_copy(targets_hbm, targets, load_sem.at[chunks + 2])
    load_centres.start()
    for j in range(chunks):
        loads(j).start()
        if j == 0:
            load_inner.start()
    load_targets.start()

    def live(k):
        return (k + 1) * sb > c * cb

    def tri_block(k):
        return tri_row.at[:, pl.ds(pl.multiple_of(k * sb, LANES), sb)]

    def inner_slot(k):
        return joined.at[:, pl.ds(pl.multiple_of(k * cb, LANES), cb)]

    if split:
        own_tri = pltpu.make_async_copy(tri, tri_block(s), tri_sem.at[0])
        own_tri.start()
        load_inner.wait()
        inner_t[...] = inner[...].T
        for k in range(n_s):
            @pl.when(jnp.logical_not(live(k)) & (k != s))
            def _():
                tri_row[:, k * sb:(k + 1) * sb] = jnp.zeros((cb, sb), jnp.float32)
    else:
        own_tri = pltpu.make_async_copy(tri, tri_row, tri_sem.at[0])
        own_tri.start()
        load_inner.wait()
        inner_t[...] = inner[...]

    load_centres.wait()
    centre_vals = centres[...]
    wide = centre_vals.astype(jnp.float32)
    centre_norms = jnp.sum(wide * wide, axis=1, keepdims=True)

    def tile(j):
        loads(j).wait()
        block = samples[j * chunk:(j + 1) * chunk, :]
        wide_block = block.astype(jnp.float32)
        norms = col_to_row(jnp.sum(wide_block * wide_block, axis=1, keepdims=True))
        crossed = lax.dot_general(centre_vals, block, (((1,), (1,)), ((), ())),
                                  preferred_element_type=jnp.float32)
        ktile[:, j * chunk:(j + 1) * chunk] = jnp.exp((2.0 * crossed - norms - centre_norms) * (1.0 / feat))

    def hop(way, j, piece=None):
        k = s - way * j
        lane = (1 - way) // 2
        where = tri_block(k)
        if piece is not None:
            rows = cb // PIECES
            where = tri_row.at[pl.ds(piece * rows, rows), pl.ds(pl.multiple_of(k * sb, LANES), sb)]
        return pltpu.make_async_remote_copy(
            src_ref=where, dst_ref=where,
            send_sem=chain_send.at[lane, j], recv_sem=chain_recv.at[lane, j],
            device_id=at(s + way, c), device_id_type=MESH)

    def inside(k):
        return (k >= 0) & (k < n_s)

    def chain_start(j):
        for way in (-1, 1):
            k = s - way * j

            @pl.when(inside(k) & inside(s + way) & live(k))
            def _():
                for piece in range(PIECES):
                    hop(way, j, piece).start()

    def chain_wait(j):
        for way in (1, -1):
            k = s - way * j
            lane = (1 - way) // 2

            @pl.when(inside(k) & live(k))
            def _():
                pltpu.make_async_copy(tri_block(k), tri_block(k), chain_recv.at[lane, j - 1]).wait()

    def chain_finish():
        for j in range(n_s - 1):
            for way in (1, -1):
                k = s - way * j

                @pl.when(inside(k) & inside(s + way) & live(k))
                def _():
                    hop(way, j).wait_send()

    def publish(buf, slot, index, kind):
        peers(kind, lambda a, b: pltpu.make_async_remote_copy(
            src_ref=buf.at[slot], dst_ref=buf.at[slot],
            send_sem=send_sem.at[index], recv_sem=recv_sem.at[index],
            device_id=at(a, b), device_id_type=MESH).start())

    def arrive(buf, index):
        rest = buf.at[pl.ds(0, buf.shape[0] - 1)]
        pltpu.make_async_copy(rest, rest, recv_sem.at[index]).wait()

    def settle(buf, index):
        rest = buf.at[pl.ds(0, buf.shape[0] - 1)]
        pltpu.make_async_copy(rest, rest, send_sem.at[index]).wait()

    def summed(buf, first=0, count=None):
        count = buf.shape[0] if count is None else count
        if count <= 32:
            acc = buf[first]
            for i in range(1, count):
                acc = acc + buf[first + i]
            return acc
        return lax.fori_loop(1, count, lambda i, acc: acc + buf[first + i], buf[first])

    def tail(value):
        return jnp.broadcast_to(value, (1, LANES))

    def square(vector):
        return jnp.sum(vector * vector, axis=1, keepdims=True)

    half = chunks // 2
    for j in range(half):
        tile(j)
    pl.semaphore_wait(barrier, n - 1)
    own_tri.wait()
    if split and JOINED:
        chain_start(0)

    def inner_copy(i):
        other = lax.rem(c + i, n_c)
        return pltpu.make_async_remote_copy(
            src_ref=inner_t.at[pl.ds(pl.multiple_of(other * part, 8), part)], dst_ref=inner_slot(c),
            send_sem=tri_sem.at[1], recv_sem=tri_sem.at[2],
            device_id=at(s, other), device_id_type=MESH)

    for i in range(1, n_c):
        inner_copy(i).start()
    own_inner = pltpu.make_async_copy(
        inner_t.at[pl.ds(pl.multiple_of(c * part, 8), part)], inner_slot(c), tri_sem.at[3])
    own_inner.start()
    for j in range(half, chunks):
        tile(j)

    load_targets.wait()
    aimed = jnp.sum(ktile[...] * targets[...], axis=1, keepdims=True)

    def over_samp(col, slot, index, between=None):
        buf = col_buf.at[slot]
        buf[s] = col_to_row(col)
        publish(buf, s, index, "samp")
        if between is not None:
            between()
        arrive(buf, index)
        return row_to_col(summed(buf))

    def own_block():
        return tri_row[:, pl.ds(pl.multiple_of(s * sb, LANES), sb)]

    def pull_blocks(col, scalar, slot, index, between=None):
        buf = rhs_buf.at[slot]
        buf[me, :, :sb] = jnp.sum(own_block() * col, axis=0, keepdims=True)
        buf[me, :, sb:] = tail(scalar)
        publish(buf, me, index, "all")
        if between is not None:
            between()
        arrive(buf, index)
        blocks = [summed(buf, k * n_c, n_c) for k in range(n_s)]
        scalar = blocks[0][:, sb:sb + 1]
        for k in range(1, n_s):
            scalar = scalar + blocks[k][:, sb:sb + 1]
        return jnp.concatenate([block[:, :sb] for block in blocks], axis=1), scalar

    def chain_step(j):
        if split and JOINED and 0 < j < n_s:
            chain_wait(j)
            if j < n_s - 1:
                chain_start(j)

    extra = 3 * ITERS + 1
    zero = jnp.zeros((1, 1), jnp.float32)
    if split:
        pulled = over_samp(aimed, 0, 0)
        rh, _ = pull_blocks(pulled, zero, 0, 1, lambda: chain_step(1))
    else:
        buf = rhs_buf.at[0]
        buf[me] = jnp.sum(tri_row[...] * aimed, axis=0, keepdims=True)
        publish(buf, me, 1, "all")
        arrive(buf, 1)
        rh = summed(buf)
    rh = rh / total_rows

    moved = inner_t.at[pl.ds(0, (n_c - 1) * part)]
    pltpu.make_async_copy(moved, moved, tri_sem.at[2]).wait()
    own_inner.wait()

    def condition(vector, buf, index, between=None):
        picked = jnp.sum(joined[...] * vector, axis=1, keepdims=True)
        buf[me, :, :total] = jnp.sum(joined[...] * picked, axis=0, keepdims=True)
        buf[me, :, total:] = tail(jnp.sum(picked * picked, axis=0, keepdims=True))
        publish(buf, me, index, "all")
        if between is not None:
            between()
        arrive(buf, index)
        got = summed(buf)
        return got[:, :total], got[:, total:total + 1]

    def rows_part(lifted, joined_rows, slot, index, between=None):
        if joined_rows:
            expanded = jnp.sum(tri_row[...] * lifted, axis=1, keepdims=True)
        else:
            lifted_ref[...] = lifted
            mine = lifted_ref[:, pl.ds(pl.multiple_of(s * sb, LANES), sb)]
            expanded = over_samp(jnp.sum(own_block() * mine, axis=1, keepdims=True), slot, index, between)
        return jnp.sum(ktile[...] * expanded, axis=0, keepdims=True)

    lifted, norm_now = condition(rh, vec_buf.at[0], 2)
    kept = jnp.zeros((1, rb), jnp.float32)
    for turn in range(ITERS - 1):
        base = 3 + 3 * turn
        rows_buf = row_buf.at[turn]
        first = split and turn == 0
        rows_buf[c] = rows_part(lifted, not first, 1, extra, (lambda: chain_step(2)) if first else None)
        publish(rows_buf, c, base, "cent")
        arrive(rows_buf, base)
        rows = summed(rows_buf)
        columns = jnp.sum(ktile[...] * rows, axis=1, keepdims=True)
        if first:
            for j in range(3, n_s):
                chain_step(j)
        if first and not FIRST_BACK_JOINED:
            columns = over_samp(columns, 2, extra + 1)
            back, scalar = pull_blocks(columns, square(rows) / n_c, 1, base + 1)
        else:
            buf = vec_buf.at[1 + 2 * turn]
            buf[me, :, :total] = jnp.sum(tri_row[...] * columns, axis=0, keepdims=True)
            buf[me, :, total:] = tail(square(rows) / n_c)
            publish(buf, me, base + 1, "all")
            arrive(buf, base + 1)
            got = summed(buf)
            back, scalar = got[:, :total], got[:, total:total + 1]
        mapped = back / total_rows + ridge_weight * lifted
        energy = scalar / total_rows + ridge_weight * square(lifted)
        step_size = norm_now / energy
        kept = kept + step_size * rows
        rh = rh - step_size * mapped
        fresh, norm_next = condition(rh, vec_buf.at[2 + 2 * turn], base + 2)
        lifted = fresh + (norm_next / norm_now) * lifted
        norm_now = norm_next

    last = 3 * ITERS
    all_buf[me] = rows_part(lifted, not split or LAST_JOINED, 3, extra + 2)
    publish(all_buf, me, last, "all")
    arrive(all_buf, last)
    if n_s <= 8:
        energy = jnp.zeros((1, 1), jnp.float32)
        for k in range(n_s):
            energy = energy + square(summed(all_buf, k * n_c, n_c))
    else:
        energy = lax.fori_loop(
            0, n_s, lambda k, acc: acc + square(summed(all_buf, k * n_c, n_c)), jnp.zeros((1, 1), jnp.float32))
    rows = summed(all_buf, s * n_c, n_c)
    step_size = norm_now / (energy / total_rows + ridge_weight * square(lifted))
    fitted[...] = kept + step_size * rows

    pltpu.make_async_copy(moved, moved, tri_sem.at[1]).wait()
    if split:
        if JOINED:
            chain_finish()
        settle(col_buf.at[0], 0)
        settle(col_buf.at[1], extra)
        if not FIRST_BACK_JOINED:
            settle(col_buf.at[2], extra + 1)
        if not LAST_JOINED:
            settle(col_buf.at[3], extra + 2)
    settle(rhs_buf.at[0], 1)
    settle(vec_buf.at[0], 2)
    for turn in range(ITERS - 1):
        base = 3 + 3 * turn
        settle(row_buf.at[turn], base)
        if split and turn == 0 and not FIRST_BACK_JOINED:
            settle(rhs_buf.at[1], base + 1)
        else:
            settle(vec_buf.at[1 + 2 * turn], base + 1)
        settle(vec_buf.at[2 + 2 * turn], base + 2)
    settle(all_buf, last)


def body(samples, targets, centres, tri_inv, inner_inv):
    n_s, n_c = lax.axis_size("samp"), lax.axis_size("cent")
    n = n_s * n_c
    rb, feat = samples.shape
    cb = centres.shape[0]
    sb = tri_inv.shape[1]
    total = sb * n_s
    split = sb % LANES == 0
    if split:
        tri, inner = tri_inv, inner_inv
    else:
        tri, inner = lax.all_gather(tri_inv, "samp", axis=1, tiled=True), inner_inv.T
    chunks = rb // min(256, rb)
    wide = total + LANES
    f32 = jnp.float32
    vmem = pl.BlockSpec(memory_space=pltpu.VMEM)
    hbm = pl.BlockSpec(memory_space=pltpu.HBM)
    out = pl.pallas_call(
        functools.partial(kernel, n_s, n_c, split),
        out_shape=jax.ShapeDtypeStruct((1, rb), f32),
        in_specs=[hbm] * 5,
        out_specs=vmem,
        scratch_shapes=[
            pltpu.VMEM((rb, feat), samples.dtype),
            pltpu.VMEM((1, rb), f32),
            pltpu.VMEM((cb, feat), centres.dtype),
            pltpu.VMEM(inner.shape, f32),
            pltpu.VMEM((cb, rb), f32),
            pltpu.VMEM((cb, total), f32),
            pltpu.VMEM((sb, cb), f32),
            pltpu.VMEM((sb // n_c, total), f32),
            pltpu.VMEM((1, total), f32),
            pltpu.VMEM((4, n_s, 1, cb), f32),
            pltpu.VMEM((2, n, 1, sb + LANES if split else total), f32),
            pltpu.VMEM((2 * ITERS - 1, n, 1, wide), f32),
            pltpu.VMEM((ITERS - 1, n_c, 1, rb), f32),
            pltpu.VMEM((n, 1, rb), f32),
            pltpu.SemaphoreType.DMA((chunks + 3,)),
            pltpu.SemaphoreType.DMA((4,)),
            pltpu.SemaphoreType.DMA((2, n_s)),
            pltpu.SemaphoreType.DMA((2, n_s)),
            pltpu.SemaphoreType.DMA((3 * ITERS + 4,)),
            pltpu.SemaphoreType.DMA((3 * ITERS + 4,)),
        ],
        compiler_params=pltpu.CompilerParams(
            collective_id=0, has_side_effects=True, vmem_limit_bytes=60 * 2 ** 20),
    )(samples, targets.reshape(1, rb), centres, tri, inner)
    return out.reshape(rb)


def solution(mesh):
    in_specs = (
        P(("groups", "samp"), None),
        P(("groups", "samp")),
        P(("groups", "cent"), None),
        P(("groups", "cent"), "samp"),
        P(("groups", "cent"), "samp"),
    )
    out_specs = P(("groups", "samp"))
    return jax.shard_map(body, mesh=mesh, in_specs=in_specs, out_specs=out_specs, check_vma=False)
```

```python
import functools
import jax
import jax.numpy as jnp
from jax import lax
from jax.experimental import pallas as pl
from jax.experimental.pallas import tpu as pltpu
from jax.sharding import PartitionSpec as P

ITERS = 2
ridge_weight = 0.01
FIRST_BACK_JOINED = True
LAST_JOINED = True
PIECES = 1
JOINED = FIRST_BACK_JOINED or LAST_JOINED
MESH = pl.DeviceIdType.MESH
LANES = 128


def row_to_col(row):
    width = row.shape[1]
    r = lax.broadcasted_iota(jnp.int32, (width, width), 0)
    c = lax.broadcasted_iota(jnp.int32, (width, width), 1)
    return jnp.sum(jnp.where(r == c, row, 0.0), axis=1, keepdims=True)


def col_to_row(col):
    width = col.shape[0]
    r = lax.broadcasted_iota(jnp.int32, (width, width), 0)
    c = lax.broadcasted_iota(jnp.int32, (width, width), 1)
    return jnp.sum(jnp.where(r == c, col, 0.0), axis=0, keepdims=True)


def kernel(n_s, n_c, split, samples_hbm, targets_hbm, centres_hbm, tri, inner_hbm, fitted,
           samples, targets, centres, inner, ktile, tri_row, inner_t, joined,
           lifted_ref, col_buf, rhs_buf, vec_buf, row_buf, all_buf,
           load_sem, tri_sem, chain_send, chain_recv, send_sem, recv_sem):
    g = lax.axis_index("groups")
    s = lax.axis_index("samp")
    c = lax.axis_index("cent")
    n = n_s * n_c
    me = s * n_c + c
    cb, feat = centres.shape
    rb = samples_hbm.shape[0]
    sb = inner_t.shape[0]
    total = tri_row.shape[1]
    part = sb // n_c
    total_rows = float(rb * n_s)
    chunk = min(256, rb)
    chunks = rb // chunk

    def at(ss, cc):
        return {"groups": g, "samp": ss, "cent": cc}

    def each(count, order, act):
        if count <= 16:
            for i in order:
                act(i)
        else:
            lax.fori_loop(1, count, lambda i, z: (act(i), z)[1], 0)

    def reach(i):
        a, b = i // n_c, i % n_c
        return (max(a, n_s - a) if a else 0) + (1 if b > 1 else 0)

    far_first = sorted(range(1, n), key=lambda i: -reach(i))

    def peers(kind, act):
        if kind == "samp":
            each(n_s, sorted(range(1, n_s), key=lambda i: -max(i, n_s - i)), lambda i: act(lax.rem(s + i, n_s), c))
        elif kind == "cent":
            each(n_c, range(1, n_c), lambda i: act(s, lax.rem(c + i, n_c)))
        else:
            each(n, far_first, lambda i: act(lax.rem(s + i // n_c, n_s), lax.rem(c + i % n_c, n_c)))

    def loads(j):
        rows = pl.ds(j * chunk, chunk)
        return pltpu.make_async_copy(samples_hbm.at[rows], samples.at[rows], load_sem.at[j])

    barrier = pltpu.get_barrier_semaphore()
    peers("all", lambda a, b: pl.semaphore_signal(barrier, inc=1, device_id=at(a, b), device_id_type=MESH))
    load_inner = pltpu.make_async_copy(inner_hbm, inner, load_sem.at[chunks])
    load_centres = pltpu.make_async_copy(centres_hbm, centres, load_sem.at[chunks + 1])
    load_targets = pltpu.make_async_copy(targets_hbm, targets, load_sem.at[chunks + 2])
    load_centres.start()
    for j in range(chunks):
        loads(j).start()
        if j == 0:
            load_inner.start()
    load_targets.start()

    def live(k):
        return (k + 1) * sb > c * cb

    def tri_block(k):
        return tri_row.at[:, pl.ds(pl.multiple_of(k * sb, LANES), sb)]

    def inner_slot(k):
        return joined.at[:, pl.ds(pl.multiple_of(k * cb, LANES), cb)]

    if split:
        own_tri = pltpu.make_async_copy(tri, tri_block(s), tri_sem.at[0])
        own_tri.start()
        load_inner.wait()
        inner_t[...] = inner[...].T
        for k in range(n_s):
            @pl.when(jnp.logical_not(live(k)) & (k != s))
            def _():
                tri_row[:, k * sb:(k + 1) * sb] = jnp.zeros((cb, sb), jnp.float32)
    else:
        own_tri = pltpu.make_async_copy(tri, tri_row, tri_sem.at[0])
        own_tri.start()
        load_inner.wait()
        inner_t[...] = inner[...]

    load_centres.wait()
    centre_vals = centres[...]
    wide = centre_vals.astype(jnp.float32)
    centre_norms = jnp.sum(wide * wide, axis=1, keepdims=True)

    def tile(j):
        loads(j).wait()
        block = samples[j * chunk:(j + 1) * chunk, :]
        wide_block = block.astype(jnp.float32)
        norms = col_to_row(jnp.sum(wide_block * wide_block, axis=1, keepdims=True))
        crossed = lax.dot_general(centre_vals, block, (((1,), (1,)), ((), ())),
                                  preferred_element_type=jnp.float32)
        ktile[:, j * chunk:(j + 1) * chunk] = jnp.exp((2.0 * crossed - norms - centre_norms) * (1.0 / feat))

    def hop(way, j, piece=None):
        k = s - way * j
        lane = (1 - way) // 2
        where = tri_block(k)
        if piece is not None:
            rows = cb // PIECES
            where = tri_row.at[pl.ds(piece * rows, rows), pl.ds(pl.multiple_of(k * sb, LANES), sb)]
        return pltpu.make_async_remote_copy(
            src_ref=where, dst_ref=where,
            send_sem=chain_send.at[lane, j], recv_sem=chain_recv.at[lane, j],
            device_id=at(s + way, c), device_id_type=MESH)

    def inside(k):
        return (k >= 0) & (k < n_s)

    def chain_start(j):
        for way in (-1, 1):
            k = s - way * j

            @pl.when(inside(k) & inside(s + way) & live(k))
            def _():
                for piece in range(PIECES):
                    hop(way, j, piece).start()

    def chain_wait(j):
        for way in (1, -1):
            k = s - way * j
            lane = (1 - way) // 2

            @pl.when(inside(k) & live(k))
            def _():
                pltpu.make_async_copy(tri_block(k), tri_block(k), chain_recv.at[lane, j - 1]).wait()

    def chain_finish():
        for j in range(n_s - 1):
            for way in (1, -1):
                k = s - way * j

                @pl.when(inside(k) & inside(s + way) & live(k))
                def _():
                    hop(way, j).wait_send()

    def publish(buf, slot, index, kind):
        peers(kind, lambda a, b: pltpu.make_async_remote_copy(
            src_ref=buf.at[slot], dst_ref=buf.at[slot],
            send_sem=send_sem.at[index], recv_sem=recv_sem.at[index],
            device_id=at(a, b), device_id_type=MESH).start())

    def arrive(buf, index):
        rest = buf.at[pl.ds(0, buf.shape[0] - 1)]
        pltpu.make_async_copy(rest, rest, recv_sem.at[index]).wait()

    def settle(buf, index):
        rest = buf.at[pl.ds(0, buf.shape[0] - 1)]
        pltpu.make_async_copy(rest, rest, send_sem.at[index]).wait()

    def summed(buf, first=0, count=None):
        count = buf.shape[0] if count is None else count
        if count <= 32:
            acc = buf[first]
            for i in range(1, count):
                acc = acc + buf[first + i]
            return acc
        return lax.fori_loop(1, count, lambda i, acc: acc + buf[first + i], buf[first])

    def tail(value):
        return jnp.broadcast_to(value, (1, LANES))

    def square(vector):
        return jnp.sum(vector * vector, axis=1, keepdims=True)

    half = 0
    for j in range(half):
        tile(j)
    pl.semaphore_wait(barrier, n - 1)
    own_tri.wait()
    if split and JOINED:
        chain_start(0)

    def inner_copy(i):
        other = lax.rem(c + i, n_c)
        return pltpu.make_async_remote_copy(
            src_ref=inner_t.at[pl.ds(pl.multiple_of(other * part, 8), part)], dst_ref=inner_slot(c),
            send_sem=tri_sem.at[1], recv_sem=tri_sem.at[2],
            device_id=at(s, other), device_id_type=MESH)

    for i in range(1, n_c):
        inner_copy(i).start()
    own_inner = pltpu.make_async_copy(
        inner_t.at[pl.ds(pl.multiple_of(c * part, 8), part)], inner_slot(c), tri_sem.at[3])
    own_inner.start()
    for j in range(half, chunks):
        tile(j)

    load_targets.wait()
    aimed = jnp.sum(ktile[...] * targets[...], axis=1, keepdims=True)

    def over_samp(col, slot, index, between=None):
        buf = col_buf.at[slot]
        buf[s] = col_to_row(col)
        publish(buf, s, index, "samp")
        if between is not None:
            between()
        arrive(buf, index)
        return row_to_col(summed(buf))

    def own_block():
        return tri_row[:, pl.ds(pl.multiple_of(s * sb, LANES), sb)]

    def pull_blocks(col, scalar, slot, index, between=None):
        buf = rhs_buf.at[slot]
        buf[me, :, :sb] = jnp.sum(own_block() * col, axis=0, keepdims=True)
        buf[me, :, sb:] = tail(scalar)
        publish(buf, me, index, "all")
        if between is not None:
            between()
        arrive(buf, index)
        blocks = [summed(buf, k * n_c, n_c) for k in range(n_s)]
        scalar = blocks[0][:, sb:sb + 1]
        for k in range(1, n_s):
            scalar = scalar + blocks[k][:, sb:sb + 1]
        return jnp.concatenate([block[:, :sb] for block in blocks], axis=1), scalar

    def chain_step(j):
        if split and JOINED and 0 < j < n_s:
            chain_wait(j)
            if j < n_s - 1:
                chain_start(j)

    extra = 3 * ITERS + 1
    zero = jnp.zeros((1, 1), jnp.float32)
    if split:
        pulled = over_samp(aimed, 0, 0)
        rh, _ = pull_blocks(pulled, zero, 0, 1, lambda: chain_step(1))
    else:
        buf = rhs_buf.at[0]
        buf[me] = jnp.sum(tri_row[...] * aimed, axis=0, keepdims=True)
        publish(buf, me, 1, "all")
        arrive(buf, 1)
        rh = summed(buf)
    rh = rh / total_rows

    moved = inner_t.at[pl.ds(0, (n_c - 1) * part)]
    pltpu.make_async_copy(moved, moved, tri_sem.at[2]).wait()
    own_inner.wait()

    def condition(vector, buf, index, between=None):
        picked = jnp.sum(joined[...] * vector, axis=1, keepdims=True)
        buf[me, :, :total] = jnp.sum(joined[...] * picked, axis=0, keepdims=True)
        buf[me, :, total:] = tail(jnp.sum(picked * picked, axis=0, keepdims=True))
        publish(buf, me, index, "all")
        if between is not None:
            between()
        arrive(buf, index)
        got = summed(buf)
        return got[:, :total], got[:, total:total + 1]

    def rows_part(lifted, joined_rows, slot, index, between=None):
        if joined_rows:
            expanded = jnp.sum(tri_row[...] * lifted, axis=1, keepdims=True)
        else:
            lifted_ref[...] = lifted
            mine = lifted_ref[:, pl.ds(pl.multiple_of(s * sb, LANES), sb)]
            expanded = over_samp(jnp.sum(own_block() * mine, axis=1, keepdims=True), slot, index, between)
        return jnp.sum(ktile[...] * expanded, axis=0, keepdims=True)

    lifted, norm_now = condition(rh, vec_buf.at[0], 2)
    kept = jnp.zeros((1, rb), jnp.float32)
    for turn in range(ITERS - 1):
        base = 3 + 3 * turn
        rows_buf = row_buf.at[turn]
        first = split and turn == 0
        rows_buf[c] = rows_part(lifted, not first, 1, extra, (lambda: chain_step(2)) if first else None)
        publish(rows_buf, c, base, "cent")
        arrive(rows_buf, base)
        rows = summed(rows_buf)
        columns = jnp.sum(ktile[...] * rows, axis=1, keepdims=True)
        if first:
            for j in range(3, n_s):
                chain_step(j)
        if first and not FIRST_BACK_JOINED:
            columns = over_samp(columns, 2, extra + 1)
            back, scalar = pull_blocks(columns, square(rows) / n_c, 1, base + 1)
        else:
            buf = vec_buf.at[1 + 2 * turn]
            buf[me, :, :total] = jnp.sum(tri_row[...] * columns, axis=0, keepdims=True)
            buf[me, :, total:] = tail(square(rows) / n_c)
            publish(buf, me, base + 1, "all")
            arrive(buf, base + 1)
            got = summed(buf)
            back, scalar = got[:, :total], got[:, total:total + 1]
        mapped = back / total_rows + ridge_weight * lifted
        energy = scalar / total_rows + ridge_weight * square(lifted)
        step_size = norm_now / energy
        kept = kept + step_size * rows
        rh = rh - step_size * mapped
        fresh, norm_next = condition(rh, vec_buf.at[2 + 2 * turn], base + 2)
        lifted = fresh + (norm_next / norm_now) * lifted
        norm_now = norm_next

    last = 3 * ITERS
    all_buf[me] = rows_part(lifted, not split or LAST_JOINED, 3, extra + 2)
    publish(all_buf, me, last, "all")
    arrive(all_buf, last)
    if n_s <= 8:
        energy = jnp.zeros((1, 1), jnp.float32)
        for k in range(n_s):
            energy = energy + square(summed(all_buf, k * n_c, n_c))
    else:
        energy = lax.fori_loop(
            0, n_s, lambda k, acc: acc + square(summed(all_buf, k * n_c, n_c)), jnp.zeros((1, 1), jnp.float32))
    rows = summed(all_buf, s * n_c, n_c)
    step_size = norm_now / (energy / total_rows + ridge_weight * square(lifted))
    fitted[...] = kept + step_size * rows

    pltpu.make_async_copy(moved, moved, tri_sem.at[1]).wait()
    if split:
        if JOINED:
            chain_finish()
        settle(col_buf.at[0], 0)
        settle(col_buf.at[1], extra)
        if not FIRST_BACK_JOINED:
            settle(col_buf.at[2], extra + 1)
        if not LAST_JOINED:
            settle(col_buf.at[3], extra + 2)
    settle(rhs_buf.at[0], 1)
    settle(vec_buf.at[0], 2)
    for turn in range(ITERS - 1):
        base = 3 + 3 * turn
        settle(row_buf.at[turn], base)
        if split and turn == 0 and not FIRST_BACK_JOINED:
            settle(rhs_buf.at[1], base + 1)
        else:
            settle(vec_buf.at[1 + 2 * turn], base + 1)
        settle(vec_buf.at[2 + 2 * turn], base + 2)
    settle(all_buf, last)


def body(samples, targets, centres, tri_inv, inner_inv):
    n_s, n_c = lax.axis_size("samp"), lax.axis_size("cent")
    n = n_s * n_c
    rb, feat = samples.shape
    cb = centres.shape[0]
    sb = tri_inv.shape[1]
    total = sb * n_s
    split = sb % LANES == 0
    if split:
        tri, inner = tri_inv, inner_inv
    else:
        tri, inner = lax.all_gather(tri_inv, "samp", axis=1, tiled=True), inner_inv.T
    chunks = rb // min(256, rb)
    wide = total + LANES
    f32 = jnp.float32
    vmem = pl.BlockSpec(memory_space=pltpu.VMEM)
    hbm = pl.BlockSpec(memory_space=pltpu.HBM)
    out = pl.pallas_call(
        functools.partial(kernel, n_s, n_c, split),
        out_shape=jax.ShapeDtypeStruct((1, rb), f32),
        in_specs=[hbm] * 5,
        out_specs=vmem,
        scratch_shapes=[
            pltpu.VMEM((rb, feat), samples.dtype),
            pltpu.VMEM((1, rb), f32),
            pltpu.VMEM((cb, feat), centres.dtype),
            pltpu.VMEM(inner.shape, f32),
            pltpu.VMEM((cb, rb), f32),
            pltpu.VMEM((cb, total), f32),
            pltpu.VMEM((sb, cb), f32),
            pltpu.VMEM((sb // n_c, total), f32),
            pltpu.VMEM((1, total), f32),
            pltpu.VMEM((4, n_s, 1, cb), f32),
            pltpu.VMEM((2, n, 1, sb + LANES if split else total), f32),
            pltpu.VMEM((2 * ITERS - 1, n, 1, wide), f32),
            pltpu.VMEM((ITERS - 1, n_c, 1, rb), f32),
            pltpu.VMEM((n, 1, rb), f32),
            pltpu.SemaphoreType.DMA((chunks + 3,)),
            pltpu.SemaphoreType.DMA((4,)),
            pltpu.SemaphoreType.DMA((2, n_s)),
            pltpu.SemaphoreType.DMA((2, n_s)),
            pltpu.SemaphoreType.DMA((3 * ITERS + 4,)),
            pltpu.SemaphoreType.DMA((3 * ITERS + 4,)),
        ],
        compiler_params=pltpu.CompilerParams(
            collective_id=0, has_side_effects=True, vmem_limit_bytes=60 * 2 ** 20),
    )(samples, targets.reshape(1, rb), centres, tri, inner)
    return out.reshape(rb)


def solution(mesh):
    in_specs = (
        P(("groups", "samp"), None),
        P(("groups", "samp")),
        P(("groups", "cent"), None),
        P(("groups", "cent"), "samp"),
        P(("groups", "cent"), "samp"),
    )
    out_specs = P(("groups", "samp"))
    return jax.shard_map(body, mesh=mesh, in_specs=in_specs, out_specs=out_specs, check_vma=False)
```
